32 devices in a mesh: group: 8 (over y, x, core), blk: 4 (over z).
Axes of the slice: x: 2, y: 2, z: 4, core: 2. Of those that a mesh axis runs over, the one named last changes fastest.
Arguments:
- informal: bfloat16 [4096, 1024], P(('group', 'blk')), may hold values from -6 to 6
- formal: bfloat16 [4096, 1024], P(('group', 'blk')), may hold values from -6 to 6
- labels: int32 [4096], P(('group', 'blk')), may hold values from 0 to 511
- temp: float32 [], replicated, may hold values from 2 to 4
- bias: float32 [], replicated, may hold values from -3 to -1
Outputs:
- loss: float32 [4096], P(('group', 'blk'))
- grad_informal: float32 [4096, 1024], P(('group', 'blk'))
- grad_formal: float32 [4096, 1024], P(('group', 'blk'))
- grad_temp: float32 [], replicated
- grad_bias: float32 [], replicated
The draws below stay inside these ranges and needn't reach their ends.
All inputs are finite; a program needn't handle non-finite values.
Results may differ from the reference program's by a relative error of at most 0.0025.
Values may be sent and summed in bfloat16 or wider, within the bound.
A program may use at most 64 MiB of HBM per device.

```python
import math
import jax
import jax.numpy as jnp
from jax import lax

D = 1024
SET = 512
BATCH = 4096


def plant(array, own_key, least, largest):
    dims = array.shape
    index_at = [jax.random.randint(jax.random.fold_in(own_key, axis), (), 0, dims[axis]) for axis in range(len(dims))]
    array = array.at[tuple(index_at)].set(least)
    longest = dims.index(max(dims))
    index_at[longest] = (index_at[longest] + 1) % dims[longest]
    return array.at[tuple(index_at)].set(largest)


def level_of(stream_key, extent, split, least, top_value):
    def one(axis_at, blocks):
        draws = jax.random.uniform(jax.random.fold_in(jax.random.fold_in(stream_key, 6), axis_at), (blocks,), jnp.float32, least / len(split), top_value / len(split))
        return jnp.repeat(jnp.exp(draws), extent[axis_at] // blocks).reshape((-1,) + (1,) * (len(extent) - axis_at - 1))

    gain = one(*split[0])
    for cut in split[1:]:
        gain = gain * one(*cut)
    return gain


def normal_values(key, shape, scale, bound, shards=(), kind=jnp.bfloat16):
    values = scale * jax.random.normal(key, shape, jnp.float32)
    if shards:
        values = values * level_of(key, shape, shards, -0.22, 0.18)
    return jnp.clip(values, -bound, bound).astype(kind)


def setup_inputs(seed: int = 0) -> dict:
    splits = jax.random.split(jax.random.key(seed), 6)
    informal = normal_values(splits[0], (BATCH, D), 1.0, 6.0, ((0, 32),))
    formal = normal_values(splits[1], (BATCH, D), 1.0, 6.0, ((0, 32),))
    labels = plant(jax.random.randint(splits[2], (BATCH,), 0, SET), jax.random.fold_in(splits[2], 1), 0, SET - 1).astype(jnp.int32)
    temp = jnp.clip(jax.random.uniform(splits[3], (), jnp.float32, 2.0, 4.0), 2.0, 4.0)
    bias = jnp.clip(jax.random.uniform(splits[4], (), jnp.float32, -3.0, -1.0), -3.0, -1.0)
    return dict(informal=informal, formal=formal, labels=labels, temp=temp, bias=bias)


def one_set(args, temp, bias):
    informal, formal, labels = args
    raw = jnp.dot(informal, formal.T, preferred_element_type=jnp.float32) / math.sqrt(D)
    logits = temp * raw + bias
    sign = jnp.where(labels[:, None] == labels[None, :], 1.0, -1.0).astype(jnp.float32)
    loss = lax.optimization_barrier(jnp.sum(jax.nn.softplus(-sign * logits), axis=1)) / SET
    slope = -sign * jax.nn.sigmoid(-sign * logits)
    weights = slope.astype(jnp.bfloat16)
    scale = temp / math.sqrt(D)
    grad_informal = scale * jnp.dot(weights, formal, preferred_element_type=jnp.float32)
    grad_formal = scale * jnp.dot(weights.T, informal, preferred_element_type=jnp.float32)
    return (loss, grad_informal, grad_formal, jnp.sum(slope * raw), jnp.sum(slope))

def reference(informal, formal, labels, temp, bias):
    nsets = BATCH // SET
    parts = (informal.reshape(nsets, SET, D), formal.reshape(nsets, SET, D), labels.reshape(nsets, SET))
    loss, grad_informal, grad_formal, temp_sums, bias_sums = lax.map(lambda a: one_set(a, temp, bias), parts)
    total = jnp.float32(BATCH) * jnp.float32(SET)
    return (loss.reshape(BATCH), grad_informal.reshape(BATCH, D), grad_formal.reshape(BATCH, D), jnp.sum(temp_sums) / total, jnp.sum(bias_sums) / total)
```

```python
import functools
import math

import jax
import jax.numpy as jnp
from jax import lax
from jax.experimental import pallas as pl
from jax.experimental.pallas import tpu as pltpu
from jax.sharding import PartitionSpec as P

MESH = pl.DeviceIdType.MESH
CHUNKS = 8
GRAINS = 2
LAG = 3


def nt_dot(a, b):
    return lax.dot_general(a, b, (((1,), (1,)), ((), ())), preferred_element_type=jnp.float32)


def tn_dot(a, b):
    return lax.dot_general(a, b, (((0,), (0,)), ((), ())), preferred_element_type=jnp.float32)


def kernel(
    n,
    ng,
    x_ref,
    y_ref,
    lab_ref,
    temp_ref,
    bias_ref,
    loss_ref,
    dx_ref,
    dy_ref,
    gtemp_ref,
    gbias_ref,
    ybuf,
    part,
    contrib,
    labbuf,
    labcol,
    loss_acc,
    temp_acc,
    bias_acc,
    sums,
    set_sums,
    all_sums,
    send_sem,
    recv_sem,
    lab_send,
    lab_recv,
    set_send,
    set_recv,
    all_send,
    all_recv,
):
    rows, width = x_ref.shape
    piece = y_ref.shape[1]
    root = math.sqrt(width)
    z = lax.axis_index("blk")
    g = lax.axis_index("group")
    temp = temp_ref[0]
    bias = bias_ref[0]
    grain = rows // GRAINS
    per_grain = CHUNKS // GRAINS

    place = (z, n - 1 - z)

    def real(d, u):
        return u if d == 0 else n - 1 - u

    def y_copy(d, p, c, own=False):
        u = place[d]
        j = z if own else real(d, u - p)
        return pltpu.make_async_remote_copy(
            src_ref=y_ref.at[c] if own else ybuf.at[j, c],
            dst_ref=ybuf.at[j, c],
            send_sem=send_sem.at[d, p, c],
            recv_sem=recv_sem.at[d, p, c],
            device_id={"blk": real(d, u + 1)},
            device_id_type=MESH,
        )

    def y_landing(d, p, c):
        block = ybuf.at[real(d, place[d] - 1 - p), c]
        return pltpu.make_async_remote_copy(
            src_ref=block,
            dst_ref=block,
            send_sem=send_sem.at[d, p, c],
            recv_sem=recv_sem.at[d, p, c],
            device_id={"blk": real(d, place[d] - 1)},
            device_id_type=MESH,
        )

    def part_copy(d, p, c):
        return pltpu.make_async_remote_copy(
            src_ref=part.at[d, p, c],
            dst_ref=part.at[d, p, c],
            send_sem=send_sem.at[d, p, c],
            recv_sem=recv_sem.at[d, p, c],
            device_id={"blk": real(d, place[d] + 1)},
            device_id_type=MESH,
        )

    def small_copy(src, slots, sends, recvs, axis, me, k, count):
        to = lax.rem(me + k, count)
        return pltpu.make_async_remote_copy(
            src_ref=src,
            dst_ref=slots.at[me],
            send_sem=sends.at[k],
            recv_sem=recvs.at[me],
            device_id={axis: to},
            device_id_type=MESH,
        )

    def small_landing(slots, sends, recvs, axis, me, k, count):
        source = lax.rem(me + k, count)
        return pltpu.make_async_remote_copy(
            src_ref=slots.at[source],
            dst_ref=slots.at[source],
            send_sem=sends.at[k],
            recv_sem=recvs.at[source],
            device_id={axis: source},
            device_id_type=MESH,
        )

    def each(count, what):
        def turn(k, carry):
            what(k)
            return carry

        lax.fori_loop(1, count, turn, 0)

    barrier = pltpu.get_barrier_semaphore()

    def greet(axis, me, count, k):
        pl.semaphore_signal(
            barrier, inc=1, device_id={axis: lax.rem(me + k, count)}, device_id_type=MESH
        )

    each(n, functools.partial(greet, "blk", z, n))
    each(ng, functools.partial(greet, "group", g, ng))
    pl.semaphore_wait(barrier, n + ng - 2)

    each(n, lambda k: small_copy(lab_ref, labbuf, lab_send, lab_recv, "blk", z, k, n).start())
    for c in range(CHUNKS):
        for d in range(2):

            @pl.when(place[d] < n - 1)
            def _():
                y_copy(d, 0, c, own=True).start()

    def column(labels):
        return jnp.transpose(jnp.broadcast_to(labels, (rows, rows)))

    def pieces(k):
        return pl.ds(pl.multiple_of(k * per_grain, per_grain), per_grain)

    def compute(y, j, k):
        at = pl.ds(pl.multiple_of(k * grain, grain), grain)
        y = y.reshape(grain, width)
        x = x_ref[...]
        raw = nt_dot(y, x) / root
        logits = temp * raw + bias
        positive = labcol[j, at] == lab_ref[...]
        turned = jnp.where(positive, -logits, logits)
        small = jnp.exp(-jnp.abs(turned))
        loss = jnp.maximum(turned, 0.0) + jnp.log1p(small)
        sigmoid = jnp.where(turned >= 0, 1.0, small) / (1.0 + small)
        slope = jnp.where(positive, -sigmoid, sigmoid)
        loss_acc[...] += loss
        temp_acc[...] += slope * raw
        bias_acc[...] += slope
        weights = slope.astype(jnp.bfloat16)
        back = jnp.dot(weights, x, preferred_element_type=jnp.float32)
        contrib[j, pieces(k)] = back.reshape(per_grain, piece, width)
        dx_ref[...] += tn_dot(weights, y)

    loss_acc[...] = jnp.zeros_like(loss_acc)
    temp_acc[...] = jnp.zeros_like(temp_acc)
    bias_acc[...] = jnp.zeros_like(bias_acc)
    dx_ref[...] = jnp.zeros_like(dx_ref)
    labcol[z] = column(lab_ref[...])
    for k in range(GRAINS):
        compute(y_ref[pl.ds(k * per_grain, per_grain)], z, k)

    def share_set():
        total = jnp.concatenate(
            [
                jnp.sum(temp_acc[...], axis=0, keepdims=True),
                jnp.sum(bias_acc[...], axis=0, keepdims=True),
                jnp.zeros((6, rows), jnp.float32),
            ],
            axis=0,
        )
        sums[0] = total
        set_sums[z] = total
        each(
            n,
            lambda k: small_copy(
                sums.at[0], set_sums, set_send, set_recv, "blk", z, k, n
            ).start(),
        )

    def share_all():
        each(n, lambda k: small_landing(set_sums, set_send, set_recv, "blk", z, k, n).wait_recv())
        total = set_sums[0]
        for j in range(1, n):
            total = total + set_sums[j]
        sums[1] = total
        all_sums[g] = total
        each(
            ng,
            lambda k: small_copy(
                sums.at[1], all_sums, all_send, all_recv, "group", g, k, ng
            ).start(),
        )

    def arrived(d, p, c):
        u = place[d]

        @pl.when(p < u)
        def _():
            y_landing(d, p, c).wait_recv()

            @pl.when(u < n - 1)
            def _():
                y_copy(d, p + 1, c).start()

        @pl.when(p > u)
        def _():
            part_copy(d, p, c).wait_recv()
            both = contrib[real(d, p), c] + part[d, p, c].astype(jnp.float32)
            part[d, p, c] = both.astype(jnp.bfloat16)
            part_copy(d, p, c).start()

        @pl.when(p == u)
        def _():
            part_copy(d, p, c).wait_recv()
            contrib[z, c] += part[d, p, c].astype(jnp.float32)

    def use(d, p, c):
        u = place[d]

        @pl.when((p < u) & (lax.rem(c + 1, per_grain) == 0))
        def _():
            k = lax.div(c, per_grain)
            j = real(d, u - 1 - p)
            compute(ybuf[j, pieces(k)], j, k)

            @pl.when(u == n - 1)
            def _():
                part[1 - d, p + 1, pieces(k)] = contrib[j, pieces(k)].astype(jnp.bfloat16)
                for i in range(per_grain):
                    part_copy(1 - d, p + 1, k * per_grain + i).start()

    def take(k):
        small_landing(labbuf, lab_send, lab_recv, "blk", z, k, n).wait_recv()
        source = lax.rem(z + k, n)
        labcol[source] = column(labbuf[source])

    each(n, take)

    lags = [jnp.minimum(LAG * jnp.maximum(u - 1, 0), CHUNKS) for u in place]
    last = jnp.maximum(lags[0], lags[1])
    computed = (n - 1) * CHUNKS + last

    def step(t, carry):
        for what in (arrived, use):
            for d in range(2):
                f = t - lags[d]

                @pl.when((place[d] > 0) & (f >= 0) & (f < n * CHUNKS))
                def _():
                    what(d, lax.div(f, CHUNKS), lax.rem(f, CHUNKS))

        @pl.when(t == computed)
        def _():
            share_set()

        @pl.when(t == computed + CHUNKS // 2)
        def _():
            share_all()

        return carry

    lax.fori_loop(0, n * CHUNKS + last, step, 0)

    scale = temp / root
    dx_ref[...] = scale * dx_ref[...]
    dy_ref[...] = scale * contrib[z].reshape(rows, width)
    loss_ref[...] = jnp.sum(loss_acc[...], axis=0, keepdims=True) / (rows * n)

    each(ng, lambda k: small_landing(all_sums, all_send, all_recv, "group", g, k, ng).wait_recv())
    total = all_sums[0]
    for j in range(1, ng):
        total = total + all_sums[j]
    pairs = float(rows * n * ng) * float(rows * n)
    gtemp_ref[0] = jnp.sum(total[0:1]) / pairs
    gbias_ref[0] = jnp.sum(total[1:2]) / pairs

    def sent(f, carry):
        p, c = lax.div(f, CHUNKS), lax.rem(f, CHUNKS)
        for d in range(2):
            u = place[d]

            @pl.when((u < n - 1) & (p <= u))
            def _():
                y_copy(d, p, c).wait_send()

            @pl.when((u < n - 1) & (p > u))
            def _():
                part_copy(d, p, c).wait_send()

        return carry

    lax.fori_loop(0, n * CHUNKS, sent, 0)
    each(n, lambda k: small_copy(lab_ref, labbuf, lab_send, lab_recv, "blk", z, k, n).wait_send())
    each(
        n,
        lambda k: small_copy(sums.at[0], set_sums, set_send, set_recv, "blk", z, k, n).wait_send(),
    )
    each(
        ng,
        lambda k: small_copy(
            sums.at[1], all_sums, all_send, all_recv, "group", g, k, ng
        ).wait_send(),
    )


def on_device(informal, formal, labels, temp, bias):
    rows, width = informal.shape
    ng = lax.axis_size("group")
    n = lax.axis_size("blk")
    vmem = pl.BlockSpec(memory_space=pltpu.VMEM)
    smem = pl.BlockSpec(memory_space=pltpu.SMEM)
    f32 = jnp.float32
    dma = pltpu.SemaphoreType.DMA
    loss, dx, dy, gtemp, gbias = pl.pallas_call(
        functools.partial(kernel, n, ng),
        out_shape=(
            jax.ShapeDtypeStruct((1, rows), f32),
            jax.ShapeDtypeStruct((rows, width), f32),
            jax.ShapeDtypeStruct((rows, width), f32),
            jax.ShapeDtypeStruct((1,), f32),
            jax.ShapeDtypeStruct((1,), f32),
        ),
        in_specs=[vmem, vmem, vmem, smem, smem],
        out_specs=(vmem, vmem, vmem, smem, smem),
        scratch_shapes=[
            pltpu.VMEM((n, CHUNKS, rows // CHUNKS, width), jnp.bfloat16),
            pltpu.VMEM((2, n, CHUNKS, rows // CHUNKS, width), jnp.bfloat16),
            pltpu.VMEM((n, CHUNKS, rows // CHUNKS, width), f32),
            pltpu.VMEM((n, 1, rows), jnp.int32),
            pltpu.VMEM((n, rows, rows), jnp.int32),
            pltpu.VMEM((rows // GRAINS, rows), f32),
            pltpu.VMEM((rows // GRAINS, rows), f32),
            pltpu.VMEM((rows // GRAINS, rows), f32),
            pltpu.VMEM((2, 8, rows), f32),
            pltpu.VMEM((n, 8, rows), f32),
            pltpu.VMEM((ng, 8, rows), f32),
            dma((2, n, CHUNKS)),
            dma((2, n, CHUNKS)),
            dma((n,)),
            dma((n,)),
            dma((n,)),
            dma((n,)),
            dma((ng,)),
            dma((ng,)),
        ],
        compiler_params=pltpu.CompilerParams(
            collective_id=0, has_side_effects=True, vmem_limit_bytes=48 * 2**20
        ),
    )(
        informal,
        formal.reshape(CHUNKS, rows // CHUNKS, width),
        labels.reshape(1, rows),
        temp.reshape(1),
        bias.reshape(1),
    )
    return loss.reshape(rows), dx, dy, gtemp.reshape(()), gbias.reshape(())


def solution(mesh):
    in_specs = (P(("group", "blk"), None), P(("group", "blk"), None), P(("group", "blk")), P(), P())
    out_specs = (
        P(("group", "blk")),
        P(("group", "blk"), None),
        P(("group", "blk"), None),
        P(),
        P(),
    )
    return jax.shard_map(
        on_device, mesh=mesh, in_specs=in_specs, out_specs=out_specs, check_vma=False
    )
```

```python
import functools
import math

import jax
import jax.numpy as jnp
from jax import lax
from jax.experimental import pallas as pl
from jax.experimental.pallas import tpu as pltpu
from jax.sharding import PartitionSpec as P

MESH = pl.DeviceIdType.MESH
CHUNKS = 8
GRAINS = 2
LAG = 3


def nt_dot(a, b):
    return lax.dot_general(a, b, (((1,), (1,)), ((), ())), preferred_element_type=jnp.float32)


def tn_dot(a, b):
    return lax.dot_general(a, b, (((0,), (0,)), ((), ())), preferred_element_type=jnp.float32)


def kernel(
    n,
    ng,
    x_ref,
    y_ref,
    lab_ref,
    temp_ref,
    bias_ref,
    loss_ref,
    dx_ref,
    dy_ref,
    gtemp_ref,
    gbias_ref,
    ybuf,
    part,
    contrib,
    labbuf,
    labcol,
    loss_acc,
    temp_acc,
    bias_acc,
    sums,
    set_sums,
    all_sums,
    send_sem,
    recv_sem,
    lab_send,
    lab_recv,
    set_send,
    set_recv,
    all_send,
    all_recv,
):
    rows, width = x_ref.shape
    piece = y_ref.shape[1]
    root = math.sqrt(width)
    z = lax.axis_index("blk")
    g = lax.axis_index("group")
    temp = temp_ref[0]
    bias = bias_ref[0]
    grain = rows // GRAINS
    per_grain = CHUNKS // GRAINS

    place = (z, n - 1 - z)

    def real(d, u):
        return u if d == 0 else n - 1 - u

    def y_copy(d, p, c, own=False):
        u = place[d]
        j = z if own else real(d, u - p)
        return pltpu.make_async_remote_copy(
            src_ref=y_ref.at[c] if own else ybuf.at[j, c],
            dst_ref=ybuf.at[j, c],
            send_sem=send_sem.at[d, p, c],
            recv_sem=recv_sem.at[d, p, c],
            device_id={"blk": real(d, u + 1)},
            device_id_type=MESH,
        )

    def y_landing(d, p, c):
        block = ybuf.at[real(d, place[d] - 1 - p), c]
        return pltpu.make_async_remote_copy(
            src_ref=block,
            dst_ref=block,
            send_sem=send_sem.at[d, p, c],
            recv_sem=recv_sem.at[d, p, c],
            device_id={"blk": real(d, place[d] - 1)},
            device_id_type=MESH,
        )

    def part_copy(d, p, c):
        return pltpu.make_async_remote_copy(
            src_ref=part.at[d, p, c],
            dst_ref=part.at[d, p, c],
            send_sem=send_sem.at[d, p, c],
            recv_sem=recv_sem.at[d, p, c],
            device_id={"blk": real(d, place[d] + 1)},
            device_id_type=MESH,
        )

    def small_copy(src, slots, sends, recvs, axis, me, k, count):
        to = lax.rem(me + k, count)
        return pltpu.make_async_remote_copy(
            src_ref=src,
            dst_ref=slots.at[me],
            send_sem=sends.at[k],
            recv_sem=recvs.at[me],
            device_id={axis: to},
            device_id_type=MESH,
        )

    def small_landing(slots, sends, recvs, axis, me, k, count):
        source = lax.rem(me + k, count)
        return pltpu.make_async_remote_copy(
            src_ref=slots.at[source],
            dst_ref=slots.at[source],
            send_sem=sends.at[k],
            recv_sem=recvs.at[source],
            device_id={axis: source},
            device_id_type=MESH,
        )

    def each(count, what):
        def turn(k, carry):
            what(k)
            return carry

        lax.fori_loop(1, count, turn, 0)

    barrier = pltpu.get_barrier_semaphore()

    def greet(axis, me, count, k):
        pl.semaphore_signal(
            barrier, inc=1, device_id={axis: lax.rem(me + k, count)}, device_id_type=MESH
        )

    each(n, functools.partial(greet, "blk", z, n))
    each(ng, functools.partial(greet, "group", g, ng))
    pl.semaphore_wait(barrier, n + ng - 2)

    each(n, lambda k: small_copy(lab_ref, labbuf, lab_send, lab_recv, "blk", z, k, n).start())
    for c in range(CHUNKS):
        for d in range(2):

            @pl.when(place[d] < n - 1)
            def _():
                y_copy(d, 0, c, own=True).start()

    def column(labels):
        return jnp.transpose(jnp.broadcast_to(labels, (rows, rows)))

    def pieces(k):
        return pl.ds(pl.multiple_of(k * per_grain, per_grain), per_grain)

    def compute(y, j, k):
        at = pl.ds(pl.multiple_of(k * grain, grain), grain)
        y = y.reshape(grain, width)
        x = x_ref[...]
        raw = nt_dot(y, x) / root
        logits = temp * raw + bias
        positive = labcol[j, at] == lab_ref[...]
        turned = jnp.where(positive, -logits, logits)
        small = jnp.exp(-jnp.abs(turned))
        loss = jnp.maximum(turned, 0.0) + jnp.log1p(small)
        sigmoid = jnp.where(turned >= 0, 1.0, small) / (1.0 + small)
        slope = jnp.where(positive, -sigmoid, sigmoid)
        loss_acc[...] += loss
        temp_acc[...] += slope * raw
        bias_acc[...] += slope
        weights = slope.astype(jnp.bfloat16)
        back = jnp.dot(weights, x, preferred_element_type=jnp.float32)
        contrib[j, pieces(k)] = back.reshape(per_grain, piece, width)
        dx_ref[...] += tn_dot(weights, y)

    loss_acc[...] = jnp.zeros_like(loss_acc)
    temp_acc[...] = jnp.zeros_like(temp_acc)
    bias_acc[...] = jnp.zeros_like(bias_acc)
    dx_ref[...] = jnp.zeros_like(dx_ref)
    labcol[z] = column(lab_ref[...])
    for k in range(GRAINS):
        compute(y_ref[pl.ds(k * per_grain, per_grain)], z, k)

    def share_set():
        total = jnp.concatenate(
            [
                jnp.sum(temp_acc[...], axis=0, keepdims=True),
                jnp.sum(bias_acc[...], axis=0, keepdims=True),
                jnp.zeros((6, rows), jnp.float32),
            ],
            axis=0,
        )
        sums[0] = total
        set_sums[z] = total
        each(
            n,
            lambda k: small_copy(
                sums.at[0], set_sums, set_send, set_recv, "blk", z, k, n
            ).start(),
        )

    def share_all():
        each(n, lambda k: small_landing(set_sums, set_send, set_recv, "blk", z, k, n).wait_recv())
        total = set_sums[0]
        for j in range(1, n):
            total = total + set_sums[j]
        sums[1] = total
        all_sums[g] = total
        each(
            ng,
            lambda k: small_copy(
                sums.at[1], all_sums, all_send, all_recv, "group", g, k, ng
            ).start(),
        )

    def arrived(d, p, c):
        u = place[d]

        @pl.when(p < u)
        def _():
            y_landing(d, p, c).wait_recv()

            @pl.when(u < n - 1)
            def _():
                y_copy(d, p + 1, c).start()

        @pl.when(p > u)
        def _():
            part_copy(d, p, c).wait_recv()
            both = contrib[real(d, p), c] + part[d, p, c].astype(jnp.float32)
            part[d, p, c] = both.astype(jnp.bfloat16)
            part_copy(d, p, c).start()

        @pl.when(p == u)
        def _():
            part_copy(d, p, c).wait_recv()
            contrib[z, c] += part[d, p, c].astype(jnp.float32)

    def use(d, p, c):
        u = place[d]

        @pl.when((p < u) & (lax.rem(c + 1, per_grain) == 0))
        def _():
            k = lax.div(c, per_grain)
            j = real(d, u - 1 - p)
            compute(ybuf[j, pieces(k)], j, k)

            @pl.when(u == n - 1)
            def _():
                part[1 - d, p + 1, pieces(k)] = contrib[j, pieces(k)].astype(jnp.bfloat16)
                for i in range(per_grain):
                    part_copy(1 - d, p + 1, k * per_grain + i).start()

    def take(k):
        small_landing(labbuf, lab_send, lab_recv, "blk", z, k, n).wait_recv()
        source = lax.rem(z + k, n)
        labcol[source] = column(labbuf[source])

    lags = [jnp.minimum(LAG * jnp.maximum(u - 1, 0), CHUNKS) for u in place]
    last = jnp.maximum(lags[0], lags[1])
    computed = (n - 1) * CHUNKS + last

    def step(t, carry):
        @pl.when(t == per_grain - 1)
        def _():
            each(n, take)

        for what in (arrived, use):
            for d in range(2):
                f = t - lags[d]

                @pl.when((place[d] > 0) & (f >= 0) & (f < n * CHUNKS))
                def _():
                    what(d, lax.div(f, CHUNKS), lax.rem(f, CHUNKS))

        @pl.when(t == computed)
        def _():
            share_set()

        @pl.when(t == computed + CHUNKS // 2)
        def _():
            share_all()

        return carry

    lax.fori_loop(0, n * CHUNKS + last, step, 0)

    scale = temp / root
    dx_ref[...] = scale * dx_ref[...]
    dy_ref[...] = scale * contrib[z].reshape(rows, width)
    loss_ref[...] = jnp.sum(loss_acc[...], axis=0, keepdims=True) / (rows * n)

    each(ng, lambda k: small_landing(all_sums, all_send, all_recv, "group", g, k, ng).wait_recv())
    total = all_sums[0]
    for j in range(1, ng):
        total = total + all_sums[j]
    pairs = float(rows * n * ng) * float(rows * n)
    gtemp_ref[0] = jnp.sum(total[0:1]) / pairs
    gbias_ref[0] = jnp.sum(total[1:2]) / pairs

    def sent(f, carry):
        p, c = lax.div(f, CHUNKS), lax.rem(f, CHUNKS)
        for d in range(2):
            u = place[d]

            @pl.when((u < n - 1) & (p <= u))
            def _():
                y_copy(d, p, c).wait_send()

            @pl.when((u < n - 1) & (p > u))
            def _():
                part_copy(d, p, c).wait_send()

        return carry

    lax.fori_loop(0, n * CHUNKS, sent, 0)
    each(n, lambda k: small_copy(lab_ref, labbuf, lab_send, lab_recv, "blk", z, k, n).wait_send())
    each(
        n,
        lambda k: small_copy(sums.at[0], set_sums, set_send, set_recv, "blk", z, k, n).wait_send(),
    )
    each(
        ng,
        lambda k: small_copy(
            sums.at[1], all_sums, all_send, all_recv, "group", g, k, ng
        ).wait_send(),
    )


def on_device(informal, formal, labels, temp, bias):
    rows, width = informal.shape
    ng = lax.axis_size("group")
    n = lax.axis_size("blk")
    vmem = pl.BlockSpec(memory_space=pltpu.VMEM)
    smem = pl.BlockSpec(memory_space=pltpu.SMEM)
    f32 = jnp.float32
    dma = pltpu.SemaphoreType.DMA
    loss, dx, dy, gtemp, gbias = pl.pallas_call(
        functools.partial(kernel, n, ng),
        out_shape=(
            jax.ShapeDtypeStruct((1, rows), f32),
            jax.ShapeDtypeStruct((rows, width), f32),
            jax.ShapeDtypeStruct((rows, width), f32),
            jax.ShapeDtypeStruct((1,), f32),
            jax.ShapeDtypeStruct((1,), f32),
        ),
        in_specs=[vmem, vmem, vmem, smem, smem],
        out_specs=(vmem, vmem, vmem, smem, smem),
        scratch_shapes=[
            pltpu.VMEM((n, CHUNKS, rows // CHUNKS, width), jnp.bfloat16),
            pltpu.VMEM((2, n, CHUNKS, rows // CHUNKS, width), jnp.bfloat16),
            pltpu.VMEM((n, CHUNKS, rows // CHUNKS, width), f32),
            pltpu.VMEM((n, 1, rows), jnp.int32),
            pltpu.VMEM((n, rows, rows), jnp.int32),
            pltpu.VMEM((rows // GRAINS, rows), f32),
            pltpu.VMEM((rows // GRAINS, rows), f32),
            pltpu.VMEM((rows // GRAINS, rows), f32),
            pltpu.VMEM((2, 8, rows), f32),
            pltpu.VMEM((n, 8, rows), f32),
            pltpu.VMEM((ng, 8, rows), f32),
            dma((2, n, CHUNKS)),
            dma((2, n, CHUNKS)),
            dma((n,)),
            dma((n,)),
            dma((n,)),
            dma((n,)),
            dma((ng,)),
            dma((ng,)),
        ],
        compiler_params=pltpu.CompilerParams(
            collective_id=0, has_side_effects=True, vmem_limit_bytes=48 * 2**20
        ),
    )(
        informal,
        formal.reshape(CHUNKS, rows // CHUNKS, width),
        labels.reshape(1, rows),
        temp.reshape(1),
        bias.reshape(1),
    )
    return loss.reshape(rows), dx, dy, gtemp.reshape(()), gbias.reshape(())


def solution(mesh):
    in_specs = (P(("group", "blk"), None), P(("group", "blk"), None), P(("group", "blk")), P(), P())
    out_specs = (
        P(("group", "blk")),
        P(("group", "blk"), None),
        P(("group", "blk"), None),
        P(),
        P(),
    )
    return jax.shard_map(
        on_device, mesh=mesh, in_specs=in_specs, out_specs=out_specs, check_vma=False
    )
```

```python
import functools
import math

import jax
import jax.numpy as jnp
from jax import lax
from jax.experimental import pallas as pl
from jax.experimental.pallas import tpu as pltpu
from jax.sharding import PartitionSpec as P

MESH = pl.DeviceIdType.MESH
CHUNKS = 8
GRAINS = 2
LAG = 3


def nt_dot(a, b):
    return lax.dot_general(a, b, (((1,), (1,)), ((), ())), preferred_element_type=jnp.float32)


def tn_dot(a, b):
    return lax.dot_general(a, b, (((0,), (0,)), ((), ())), preferred_element_type=jnp.float32)


def kernel(
    n,
    ng,
    x_ref,
    y_ref,
    lab_ref,
    temp_ref,
    bias_ref,
    loss_ref,
    dx_ref,
    dy_ref,
    gtemp_ref,
    gbias_ref,
    ybuf,
    part,
    contrib,
    labbuf,
    labcol,
    loss_acc,
    temp_acc,
    bias_acc,
    sums,
    set_sums,
    all_sums,
    send_sem,
    recv_sem,
    lab_send,
    lab_recv,
    set_send,
    set_recv,
    all_send,
    all_recv,
):
    rows, width = x_ref.shape
    piece = y_ref.shape[1]
    root = math.sqrt(width)
    z = lax.axis_index("blk")
    g = lax.axis_index("group")
    temp = temp_ref[0]
    bias = bias_ref[0]
    grain = rows // GRAINS
    per_grain = CHUNKS // GRAINS

    place = (z, n - 1 - z)

    def real(d, u):
        return u if d == 0 else n - 1 - u

    def y_copy(d, p, c, own=False):
        u = place[d]
        j = z if own else real(d, u - p)
        return pltpu.make_async_remote_copy(
            src_ref=y_ref.at[c] if own else ybuf.at[j, c],
            dst_ref=ybuf.at[j, c],
            send_sem=send_sem.at[d, p, c],
            recv_sem=recv_sem.at[d, p, c],
            device_id={"blk": real(d, u + 1)},
            device_id_type=MESH,
        )

    def y_landing(d, p, c):
        block = ybuf.at[real(d, place[d] - 1 - p), c]
        return pltpu.make_async_remote_copy(
            src_ref=block,
            dst_ref=block,
            send_sem=send_sem.at[d, p, c],
            recv_sem=recv_sem.at[d, p, c],
            device_id={"blk": real(d, place[d] - 1)},
            device_id_type=MESH,
        )

    def part_copy(d, p, c):
        return pltpu.make_async_remote_copy(
            src_ref=part.at[d, p, c],
            dst_ref=part.at[d, p, c],
            send_sem=send_sem.at[d, p, c],
            recv_sem=recv_sem.at[d, p, c],
            device_id={"blk": real(d, place[d] + 1)},
            device_id_type=MESH,
        )

    def small_copy(src, slots, sends, recvs, axis, me, k, count):
        to = lax.rem(me + k, count)
        return pltpu.make_async_remote_copy(
            src_ref=src,
            dst_ref=slots.at[me],
            send_sem=sends.at[k],
            recv_sem=recvs.at[me],
            device_id={axis: to},
            device_id_type=MESH,
        )

    def small_landing(slots, sends, recvs, axis, me, k, count):
        source = lax.rem(me + k, count)
        return pltpu.make_async_remote_copy(
            src_ref=slots.at[source],
            dst_ref=slots.at[source],
            send_sem=sends.at[k],
            recv_sem=recvs.at[source],
            device_id={axis: source},
            device_id_type=MESH,
        )

    def each(count, what):
        def turn(k, carry):
            what(k)
            return carry

        lax.fori_loop(1, count, turn, 0)

    rounds = ng.bit_length() - 1
    assert ng == 1 << rounds

    def mate(r):
        return g + (1 << r) * (1 - 2 * lax.rem(lax.div(g, 1 << r), 2))

    def pair_copy(r):
        return pltpu.make_async_remote_copy(
            src_ref=sums.at[1 + r],
            dst_ref=all_sums.at[r],
            send_sem=all_send.at[r],
            recv_sem=all_recv.at[r],
            device_id={"group": mate(r)},
            device_id_type=MESH,
        )

    barrier = pltpu.get_barrier_semaphore()

    def greet(axis, me, count, k):
        pl.semaphore_signal(
            barrier, inc=1, device_id={axis: lax.rem(me + k, count)}, device_id_type=MESH
        )

    each(n, functools.partial(greet, "blk", z, n))
    for r in range(rounds):
        pl.semaphore_signal(barrier, inc=1, device_id={"group": mate(r)}, device_id_type=MESH)
    pl.semaphore_wait(barrier, n - 1 + rounds)

    each(n, lambda k: small_copy(lab_ref, labbuf, lab_send, lab_recv, "blk", z, k, n).start())
    for c in range(CHUNKS):
        for d in range(2):

            @pl.when(place[d] < n - 1)
            def _():
                y_copy(d, 0, c, own=True).start()

    def column(labels):
        return jnp.transpose(jnp.broadcast_to(labels, (rows, rows)))

    def pieces(k):
        return pl.ds(pl.multiple_of(k * per_grain, per_grain), per_grain)

    def compute(y, j, k):
        at = pl.ds(pl.multiple_of(k * grain, grain), grain)
        y = y.reshape(grain, width)
        x = x_ref[...]
        raw = nt_dot(y, x) / root
        logits = temp * raw + bias
        positive = labcol[j, at] == lab_ref[...]
        turned = jnp.where(positive, -logits, logits)
        small = jnp.exp(-jnp.abs(turned))
        loss = jnp.maximum(turned, 0.0) + jnp.log1p(small)
        sigmoid = jnp.where(turned >= 0, 1.0, small) / (1.0 + small)
        slope = jnp.where(positive, -sigmoid, sigmoid)
        loss_acc[...] += loss
        temp_acc[...] += slope * raw
        bias_acc[...] += slope
        weights = slope.astype(jnp.bfloat16)
        back = jnp.dot(weights, x, preferred_element_type=jnp.float32)
        contrib[j, pieces(k)] = back.reshape(per_grain, piece, width)
        dx_ref[...] += tn_dot(weights, y)

    loss_acc[...] = jnp.zeros_like(loss_acc)
    temp_acc[...] = jnp.zeros_like(temp_acc)
    bias_acc[...] = jnp.zeros_like(bias_acc)
    dx_ref[...] = jnp.zeros_like(dx_ref)
    labcol[z] = column(lab_ref[...])
    for k in range(GRAINS):
        compute(y_ref[pl.ds(k * per_grain, per_grain)], z, k)

    def share_set():
        total = jnp.concatenate(
            [
                jnp.sum(temp_acc[...], axis=0, keepdims=True),
                jnp.sum(bias_acc[...], axis=0, keepdims=True),
                jnp.zeros((6, rows), jnp.float32),
            ],
            axis=0,
        )
        sums[0] = total
        set_sums[z] = total
        each(
            n,
            lambda k: small_copy(
                sums.at[0], set_sums, set_send, set_recv, "blk", z, k, n
            ).start(),
        )

    def share_all():
        each(n, lambda k: small_landing(set_sums, set_send, set_recv, "blk", z, k, n).wait_recv())
        total = set_sums[0]
        for j in range(1, n):
            total = total + set_sums[j]
        sums[1] = total
        pair_copy(0).start()

    def join(r):
        pair_copy(r - 1).wait_recv()
        sums[1 + r] = sums[r] + all_sums[r - 1]
        if r < rounds:
            pair_copy(r).start()

    def arrived(d, p, c):
        u = place[d]

        @pl.when(p < u)
        def _():
            y_landing(d, p, c).wait_recv()

            @pl.when(u < n - 1)
            def _():
                y_copy(d, p + 1, c).start()

        @pl.when(p > u)
        def _():
            part_copy(d, p, c).wait_recv()
            both = contrib[real(d, p), c] + part[d, p, c].astype(jnp.float32)
            part[d, p, c] = both.astype(jnp.bfloat16)
            part_copy(d, p, c).start()

        @pl.when(p == u)
        def _():
            part_copy(d, p, c).wait_recv()
            contrib[z, c] += part[d, p, c].astype(jnp.float32)

    def use(d, p, c):
        u = place[d]

        @pl.when((p < u) & (lax.rem(c + 1, per_grain) == 0))
        def _():
            k = lax.div(c, per_grain)
            j = real(d, u - 1 - p)
            compute(ybuf[j, pieces(k)], j, k)

            @pl.when(u == n - 1)
            def _():
                part[1 - d, p + 1, pieces(k)] = contrib[j, pieces(k)].astype(jnp.bfloat16)
                for i in range(per_grain):
                    part_copy(1 - d, p + 1, k * per_grain + i).start()

    def take(k):
        small_landing(labbuf, lab_send, lab_recv, "blk", z, k, n).wait_recv()
        source = lax.rem(z + k, n)
        labcol[source] = column(labbuf[source])

    each(n, take)

    lags = [jnp.minimum(LAG * jnp.maximum(u - 1, 0), CHUNKS) for u in place]
    last = jnp.maximum(lags[0], lags[1])
    computed = (n - 1) * CHUNKS + last

    def step(t, carry):
        for what in (arrived, use):
            for d in range(2):
                f = t - lags[d]

                @pl.when((place[d] > 0) & (f >= 0) & (f < n * CHUNKS))
                def _():
                    what(d, lax.div(f, CHUNKS), lax.rem(f, CHUNKS))

        @pl.when(t == computed)
        def _():
            share_set()

        for r in range(rounds):

            @pl.when(t == computed + min(2 + 2 * r, CHUNKS - 1))
            def _():
                if r == 0:
                    share_all()
                else:
                    join(r)

        return carry

    lax.fori_loop(0, n * CHUNKS + last, step, 0)

    scale = temp / root
    dx_ref[...] = scale * dx_ref[...]
    dy_ref[...] = scale * contrib[z].reshape(rows, width)
    loss_ref[...] = jnp.sum(loss_acc[...], axis=0, keepdims=True) / (rows * n)

    join(rounds)
    total = sums[1 + rounds]
    pairs = float(rows * n * ng) * float(rows * n)
    gtemp_ref[0] = jnp.sum(total[0:1]) / pairs
    gbias_ref[0] = jnp.sum(total[1:2]) / pairs

    def sent(f, carry):
        p, c = lax.div(f, CHUNKS), lax.rem(f, CHUNKS)
        for d in range(2):
            u = place[d]

            @pl.when((u < n - 1) & (p <= u))
            def _():
                y_copy(d, p, c).wait_send()

            @pl.when((u < n - 1) & (p > u))
            def _():
                part_copy(d, p, c).wait_send()

        return carry

    lax.fori_loop(0, n * CHUNKS, sent, 0)
    each(n, lambda k: small_copy(lab_ref, labbuf, lab_send, lab_recv, "blk", z, k, n).wait_send())
    each(
        n,
        lambda k: small_copy(sums.at[0], set_sums, set_send, set_recv, "blk", z, k, n).wait_send(),
    )
    for r in range(rounds):
        pair_copy(r).wait_send()


def on_device(informal, formal, labels, temp, bias):
    rows, width = informal.shape
    ng = lax.axis_size("group")
    n = lax.axis_size("blk")
    vmem = pl.BlockSpec(memory_space=pltpu.VMEM)
    smem = pl.BlockSpec(memory_space=pltpu.SMEM)
    f32 = jnp.float32
    dma = pltpu.SemaphoreType.DMA
    loss, dx, dy, gtemp, gbias = pl.pallas_call(
        functools.partial(kernel, n, ng),
        out_shape=(
            jax.ShapeDtypeStruct((1, rows), f32),
            jax.ShapeDtypeStruct((rows, width), f32),
            jax.ShapeDtypeStruct((rows, width), f32),
            jax.ShapeDtypeStruct((1,), f32),
            jax.ShapeDtypeStruct((1,), f32),
        ),
        in_specs=[vmem, vmem, vmem, smem, smem],
        out_specs=(vmem, vmem, vmem, smem, smem),
        scratch_shapes=[
            pltpu.VMEM((n, CHUNKS, rows // CHUNKS, width), jnp.bfloat16),
            pltpu.VMEM((2, n, CHUNKS, rows // CHUNKS, width), jnp.bfloat16),
            pltpu.VMEM((n, CHUNKS, rows // CHUNKS, width), f32),
            pltpu.VMEM((n, 1, rows), jnp.int32),
            pltpu.VMEM((n, rows, rows), jnp.int32),
            pltpu.VMEM((rows // GRAINS, rows), f32),
            pltpu.VMEM((rows // GRAINS, rows), f32),
            pltpu.VMEM((rows // GRAINS, rows), f32),
            pltpu.VMEM((ng.bit_length() + 1, 8, rows), f32),
            pltpu.VMEM((n, 8, rows), f32),
            pltpu.VMEM((ng, 8, rows), f32),
            dma((2, n, CHUNKS)),
            dma((2, n, CHUNKS)),
            dma((n,)),
            dma((n,)),
            dma((n,)),
            dma((n,)),
            dma((ng,)),
            dma((ng,)),
        ],
        compiler_params=pltpu.CompilerParams(
            collective_id=0, has_side_effects=True, vmem_limit_bytes=48 * 2**20
        ),
    )(
        informal,
        formal.reshape(CHUNKS, rows // CHUNKS, width),
        labels.reshape(1, rows),
        temp.reshape(1),
        bias.reshape(1),
    )
    return loss.reshape(rows), dx, dy, gtemp.reshape(()), gbias.reshape(())


def solution(mesh):
    in_specs = (P(("group", "blk"), None), P(("group", "blk"), None), P(("group", "blk")), P(), P())
    out_specs = (
        P(("group", "blk")),
        P(("group", "blk"), None),
        P(("group", "blk"), None),
        P(),
        P(),
    )
    return jax.shard_map(
        on_device, mesh=mesh, in_specs=in_specs, out_specs=out_specs, check_vma=False
    )
```

```python
import functools
import math

import jax
import jax.numpy as jnp
from jax import lax
from jax.experimental import pallas as pl
from jax.experimental.pallas import tpu as pltpu
from jax.sharding import PartitionSpec as P

MESH = pl.DeviceIdType.MESH
CHUNKS = 8
GRAINS = 2
LAG = 2


def nt_dot(a, b):
    return lax.dot_general(a, b, (((1,), (1,)), ((), ())), preferred_element_type=jnp.float32)


def tn_dot(a, b):
    return lax.dot_general(a, b, (((0,), (0,)), ((), ())), preferred_element_type=jnp.float32)


def kernel(
    n,
    ng,
    x_ref,
    y_ref,
    lab_ref,
    temp_ref,
    bias_ref,
    loss_ref,
    dx_ref,
    dy_ref,
    gtemp_ref,
    gbias_ref,
    ybuf,
    part,
    contrib,
    labbuf,
    labcol,
    loss_acc,
    temp_acc,
    bias_acc,
    sums,
    set_sums,
    all_sums,
    send_sem,
    recv_sem,
    lab_send,
    lab_recv,
    set_send,
    set_recv,
    all_send,
    all_recv,
):
    rows, width = x_ref.shape
    piece = y_ref.shape[1]
    root = math.sqrt(width)
    z = lax.axis_index("blk")
    g = lax.axis_index("group")
    temp = temp_ref[0]
    bias = bias_ref[0]
    grain = rows // GRAINS
    per_grain = CHUNKS // GRAINS

    place = (z, n - 1 - z)

    def real(d, u):
        return u if d == 0 else n - 1 - u

    def y_copy(d, p, c, own=False):
        u = place[d]
        j = z if own else real(d, u - p)
        return pltpu.make_async_remote_copy(
            src_ref=y_ref.at[c] if own else ybuf.at[j, c],
            dst_ref=ybuf.at[j, c],
            send_sem=send_sem.at[d, p, c],
            recv_sem=recv_sem.at[d, p, c],
            device_id={"blk": real(d, u + 1)},
            device_id_type=MESH,
        )

    def y_landing(d, p, c):
        block = ybuf.at[real(d, place[d] - 1 - p), c]
        return pltpu.make_async_remote_copy(
            src_ref=block,
            dst_ref=block,
            send_sem=send_sem.at[d, p, c],
            recv_sem=recv_sem.at[d, p, c],
            device_id={"blk": real(d, place[d] - 1)},
            device_id_type=MESH,
        )

    def part_copy(d, p, c):
        return pltpu.make_async_remote_copy(
            src_ref=part.at[d, p, c],
            dst_ref=part.at[d, p, c],
            send_sem=send_sem.at[d, p, c],
            recv_sem=recv_sem.at[d, p, c],
            device_id={"blk": real(d, place[d] + 1)},
            device_id_type=MESH,
        )

    def small_copy(src, slots, sends, recvs, axis, me, k, count):
        to = lax.rem(me + k, count)
        return pltpu.make_async_remote_copy(
            src_ref=src,
            dst_ref=slots.at[me],
            send_sem=sends.at[k],
            recv_sem=recvs.at[me],
            device_id={axis: to},
            device_id_type=MESH,
        )

    def small_landing(slots, sends, recvs, axis, me, k, count):
        source = lax.rem(me + k, count)
        return pltpu.make_async_remote_copy(
            src_ref=slots.at[source],
            dst_ref=slots.at[source],
            send_sem=sends.at[k],
            recv_sem=recvs.at[source],
            device_id={axis: source},
            device_id_type=MESH,
        )

    def each(count, what):
        def turn(k, carry):
            what(k)
            return carry

        lax.fori_loop(1, count, turn, 0)

    barrier = pltpu.get_barrier_semaphore()

    def greet(axis, me, count, k):
        pl.semaphore_signal(
            barrier, inc=1, device_id={axis: lax.rem(me + k, count)}, device_id_type=MESH
        )

    each(n, functools.partial(greet, "blk", z, n))
    each(ng, functools.partial(greet, "group", g, ng))
    pl.semaphore_wait(barrier, n + ng - 2)

    each(n, lambda k: small_copy(lab_ref, labbuf, lab_send, lab_recv, "blk", z, k, n).start())
    for c in range(CHUNKS):
        for d in range(2):

            @pl.when(place[d] < n - 1)
            def _():
                y_copy(d, 0, c, own=True).start()

    def column(labels):
        return jnp.transpose(jnp.broadcast_to(labels, (rows, rows)))

    def pieces(k):
        return pl.ds(pl.multiple_of(k * per_grain, per_grain), per_grain)

    def compute(y, j, k):
        at = pl.ds(pl.multiple_of(k * grain, grain), grain)
        y = y.reshape(grain, width)
        x = x_ref[...]
        raw = nt_dot(y, x) / root
        logits = temp * raw + bias
        positive = labcol[j, at] == lab_ref[...]
        turned = jnp.where(positive, -logits, logits)
        small = jnp.exp(-jnp.abs(turned))
        loss = jnp.maximum(turned, 0.0) + jnp.log1p(small)
        sigmoid = jnp.where(turned >= 0, 1.0, small) / (1.0 + small)
        slope = jnp.where(positive, -sigmoid, sigmoid)
        loss_acc[...] += loss
        temp_acc[...] += slope * raw
        bias_acc[...] += slope
        weights = slope.astype(jnp.bfloat16)
        back = jnp.dot(weights, x, preferred_element_type=jnp.float32)
        contrib[j, pieces(k)] = back.reshape(per_grain, piece, width)
        dx_ref[...] += tn_dot(weights, y)

    loss_acc[...] = jnp.zeros_like(loss_acc)
    temp_acc[...] = jnp.zeros_like(temp_acc)
    bias_acc[...] = jnp.zeros_like(bias_acc)
    dx_ref[...] = jnp.zeros_like(dx_ref)
    labcol[z] = column(lab_ref[...])
    for k in range(GRAINS):
        compute(y_ref[pl.ds(k * per_grain, per_grain)], z, k)

    def share_set():
        total = jnp.concatenate(
            [
                jnp.sum(temp_acc[...], axis=0, keepdims=True),
                jnp.sum(bias_acc[...], axis=0, keepdims=True),
                jnp.zeros((6, rows), jnp.float32),
            ],
            axis=0,
        )
        sums[0] = total
        set_sums[z] = total
        each(
            n,
            lambda k: small_copy(
                sums.at[0], set_sums, set_send, set_recv, "blk", z, k, n
            ).start(),
        )

    def share_all():
        each(n, lambda k: small_landing(set_sums, set_send, set_recv, "blk", z, k, n).wait_recv())
        total = set_sums[0]
        for j in range(1, n):
            total = total + set_sums[j]
        sums[1] = total
        all_sums[g] = total
        each(
            ng,
            lambda k: small_copy(
                sums.at[1], all_sums, all_send, all_recv, "group", g, k, ng
            ).start(),
        )

    def arrived(d, p, c):
        u = place[d]

        @pl.when(p < u)
        def _():
            y_landing(d, p, c).wait_recv()

            @pl.when(u < n - 1)
            def _():
                y_copy(d, p + 1, c).start()

        @pl.when(p > u)
        def _():
            part_copy(d, p, c).wait_recv()
            both = contrib[real(d, p), c] + part[d, p, c].astype(jnp.float32)
            part[d, p, c] = both.astype(jnp.bfloat16)
            part_copy(d, p, c).start()

        @pl.when(p == u)
        def _():
            part_copy(d, p, c).wait_recv()
            contrib[z, c] += part[d, p, c].astype(jnp.float32)

    def use(d, p, c):
        u = place[d]

        @pl.when((p < u) & (lax.rem(c + 1, per_grain) == 0))
        def _():
            k = lax.div(c, per_grain)
            j = real(d, u - 1 - p)
            compute(ybuf[j, pieces(k)], j, k)

            @pl.when(u == n - 1)
            def _():
                part[1 - d, p + 1, pieces(k)] = contrib[j, pieces(k)].astype(jnp.bfloat16)
                for i in range(per_grain):
                    part_copy(1 - d, p + 1, k * per_grain + i).start()

    def take(k):
        small_landing(labbuf, lab_send, lab_recv, "blk", z, k, n).wait_recv()
        source = lax.rem(z + k, n)
        labcol[source] = column(labbuf[source])

    each(n, take)

    lags = [jnp.minimum(LAG * jnp.maximum(u - 1, 0), CHUNKS) for u in place]
    last = jnp.maximum(lags[0], lags[1])
    computed = (n - 1) * CHUNKS + last

    def step(t, carry):
        for what in (arrived, use):
            for d in range(2):
                f = t - lags[d]

                @pl.when((place[d] > 0) & (f >= 0) & (f < n * CHUNKS))
                def _():
                    what(d, lax.div(f, CHUNKS), lax.rem(f, CHUNKS))

        @pl.when(t == computed)
        def _():
            share_set()

        @pl.when(t == computed + CHUNKS // 2)
        def _():
            share_all()

        return carry

    lax.fori_loop(0, n * CHUNKS + last, step, 0)

    scale = temp / root
    dx_ref[...] = scale * dx_ref[...]
    dy_ref[...] = scale * contrib[z].reshape(rows, width)
    loss_ref[...] = jnp.sum(loss_acc[...], axis=0, keepdims=True) / (rows * n)

    each(ng, lambda k: small_landing(all_sums, all_send, all_recv, "group", g, k, ng).wait_recv())
    total = all_sums[0]
    for j in range(1, ng):
        total = total + all_sums[j]
    pairs = float(rows * n * ng) * float(rows * n)
    gtemp_ref[0] = jnp.sum(total[0:1]) / pairs
    gbias_ref[0] = jnp.sum(total[1:2]) / pairs

    def sent(f, carry):
        p, c = lax.div(f, CHUNKS), lax.rem(f, CHUNKS)
        for d in range(2):
            u = place[d]

            @pl.when((u < n - 1) & (p <= u))
            def _():
                y_copy(d, p, c).wait_send()

            @pl.when((u < n - 1) & (p > u))
            def _():
                part_copy(d, p, c).wait_send()

        return carry

    lax.fori_loop(0, n * CHUNKS, sent, 0)
    each(n, lambda k: small_copy(lab_ref, labbuf, lab_send, lab_recv, "blk", z, k, n).wait_send())
    each(
        n,
        lambda k: small_copy(sums.at[0], set_sums, set_send, set_recv, "blk", z, k, n).wait_send(),
    )
    each(
        ng,
        lambda k: small_copy(
            sums.at[1], all_sums, all_send, all_recv, "group", g, k, ng
        ).wait_send(),
    )


def on_device(informal, formal, labels, temp, bias):
    rows, width = informal.shape
    ng = lax.axis_size("group")
    n = lax.axis_size("blk")
    vmem = pl.BlockSpec(memory_space=pltpu.VMEM)
    smem = pl.BlockSpec(memory_space=pltpu.SMEM)
    f32 = jnp.float32
    dma = pltpu.SemaphoreType.DMA
    loss, dx, dy, gtemp, gbias = pl.pallas_call(
        functools.partial(kernel, n, ng),
        out_shape=(
            jax.ShapeDtypeStruct((1, rows), f32),
            jax.ShapeDtypeStruct((rows, width), f32),
            jax.ShapeDtypeStruct((rows, width), f32),
            jax.ShapeDtypeStruct((1,), f32),
            jax.ShapeDtypeStruct((1,), f32),
        ),
        in_specs=[vmem, vmem, vmem, smem, smem],
        out_specs=(vmem, vmem, vmem, smem, smem),
        scratch_shapes=[
            pltpu.VMEM((n, CHUNKS, rows // CHUNKS, width), jnp.bfloat16),
            pltpu.VMEM((2, n, CHUNKS, rows // CHUNKS, width), jnp.bfloat16),
            pltpu.VMEM((n, CHUNKS, rows // CHUNKS, width), f32),
            pltpu.VMEM((n, 1, rows), jnp.int32),
            pltpu.VMEM((n, rows, rows), jnp.int32),
            pltpu.VMEM((rows // GRAINS, rows), f32),
            pltpu.VMEM((rows // GRAINS, rows), f32),
            pltpu.VMEM((rows // GRAINS, rows), f32),
            pltpu.VMEM((2, 8, rows), f32),
            pltpu.VMEM((n, 8, rows), f32),
            pltpu.VMEM((ng, 8, rows), f32),
            dma((2, n, CHUNKS)),
            dma((2, n, CHUNKS)),
            dma((n,)),
            dma((n,)),
            dma((n,)),
            dma((n,)),
            dma((ng,)),
            dma((ng,)),
        ],
        compiler_params=pltpu.CompilerParams(
            collective_id=0, has_side_effects=True, vmem_limit_bytes=48 * 2**20
        ),
    )(
        informal,
        formal.reshape(CHUNKS, rows // CHUNKS, width),
        labels.reshape(1, rows),
        temp.reshape(1),
        bias.reshape(1),
    )
    return loss.reshape(rows), dx, dy, gtemp.reshape(()), gbias.reshape(())


def solution(mesh):
    in_specs = (P(("group", "blk"), None), P(("group", "blk"), None), P(("group", "blk")), P(), P())
    out_specs = (
        P(("group", "blk")),
        P(("group", "blk"), None),
        P(("group", "blk"), None),
        P(),
        P(),
    )
    return jax.shard_map(
        on_device, mesh=mesh, in_specs=in_specs, out_specs=out_specs, check_vma=False
    )
```
